32 devices in a mesh: tm: 16 (over z, x, core), space: 2 (over y).
Axes of the slice: x: 2, y: 2, z: 4, core: 2. Of those that a mesh axis runs over, the one named last changes fastest.
Arguments:
- state: bfloat16 [16, 32, 64, 128], P('tm', 'space'), may hold values from -4 to 4
- initial: bfloat16 [32, 64, 128], P('space'), may hold values from -4 to 4
- forcing: bfloat16 [16, 32, 64, 128], P('tm', 'space'), may hold values from -5 to 5
- kappa: bfloat16 [32, 64, 128], P('space'), may hold values from 0.5 to 2
- reaction: bfloat16 [32, 64, 128], P('space'), may hold values from 0.019897461 to 0.19921875
Outputs:
- updated: bfloat16 [16, 32, 64, 128], P('tm', 'space')
The draws below stay inside these ranges and needn't reach their ends.
All inputs are finite; a program needn't handle non-finite values.
Results may differ from the reference program's by a relative error of at most 0.006.
The reference program's roundings to bfloat16 on the way (of `previous`, `residual` and `correction`) count: a program that leaves them out, or rounds other values in their place, can miss the bound.
Values may be sent and summed in bfloat16 or wider, within the bound.
A program may use at most 64 MiB of HBM per device.

```python
import math
import jax
import jax.numpy as jnp
from jax import lax

NY = 64
NZ = 128
SWEEPS = 6
STEPS = 16
NX = 32


def draw_forcing(key, part):
    rough = jnp.clip(jax.random.normal(key, (STEPS, NX, NY, NZ), jnp.float32), -4.0, 4.0)
    return rough.astype(jnp.bfloat16)


def levels(key, dims, pieces, smallest, largest):
    factor_of, own = 1.0, jax.random.fold_in(key, 6)
    for position, blocks in pieces:
        draws = jnp.exp(jax.random.uniform(jax.random.fold_in(own, position), (blocks,), jnp.float32, smallest / len(pieces), largest / len(pieces)))
        factor_of = factor_of * jnp.repeat(draws, dims[position] // blocks).reshape([-1 if axis == position else 1 for axis in range(len(dims))])
    return factor_of


def bell_draw(key, shape, width, most, cuts=(), held_as=jnp.bfloat16):
    drawn = width * jax.random.normal(key, shape, jnp.float32)
    if cuts:
        drawn = drawn * levels(key, shape, cuts, -0.22, 0.18)
    return jnp.clip(drawn, -most, most).astype(held_as)


def setup_inputs(seed: int = 0) -> dict:
    splits = jax.random.split(jax.random.key(seed), 6)
    state = bell_draw(splits[0], (STEPS, NX, NY, NZ), 1.0, 4.0, ((0, 16), (1, 2)))
    initial = bell_draw(splits[1], (NX, NY, NZ), 1.0, 4.0, ((0, 2),))
    forcing = draw_forcing(jax.random.fold_in(splits[5], 71), 0)
    kappa = jnp.clip(jnp.exp(math.log(2.0) - 1.3862944 * jax.random.uniform(splits[3], (NX, NY, NZ), jnp.float32) ** levels(splits[3], (NX, NY, NZ), ((0, 2),), -0.2, 0.2)), 0.5, 2.0).astype(jnp.bfloat16)
    reaction = jnp.clip(jnp.exp(math.log(0.19921875) - 2.3038113 * jax.random.uniform(splits[4], (NX, NY, NZ), jnp.float32) ** levels(splits[4], (NX, NY, NZ), ((0, 2),), -0.2, 0.2)), 0.019897461, 0.19921875).astype(jnp.bfloat16)
    return {"state": state, "initial": initial, "forcing": forcing, "kappa": kappa, "reaction": reaction}


alpha_ratio = 0.25
near_weight = 0.5
far_weight = 1.0
centre_weight = 6.0 * (near_weight + far_weight)
highest = lax.Precision.HIGHEST


def shifted(values, axis_number, offset):
    extent = values.shape[axis_number]
    widths = [(0, 0)] * values.ndim
    widths[axis_number] = (2, 2)
    padded = jnp.pad(values, widths)
    return lax.slice_in_dim(padded, 2 + offset, 2 + offset + extent, axis=axis_number)


def cycle_sums(values):
    leading = values.ndim - 3
    near_sum = shifted(values, leading, 1) + shifted(values, leading, -1)
    far_sum = shifted(values, leading, 2) + shifted(values, leading, -2)
    for axis_number in (leading + 1, leading + 2):
        near_sum = near_sum + shifted(values, axis_number, 1) + shifted(values, axis_number, -1)
        far_sum = far_sum + shifted(values, axis_number, 2) + shifted(values, axis_number, -2)
    return near_sum, far_sum


def residual_of(centre, near_sum, far_sum, before, source_term, kappa_part, reaction_part):
    return (source_term - centre + before
            - kappa_part * (centre_weight * centre - near_weight * near_sum - far_weight * far_sum)
            - reaction_part * centre * centre * centre)


def tables(length):
    counter = jnp.arange(length, dtype=jnp.int32)
    product = (counter[:, None] * counter[None, :]) % length
    angles = product.astype(jnp.float32) * (2.0 * math.pi / length)
    scaling = jnp.exp(counter.astype(jnp.float32) * (math.log(alpha_ratio) / length))
    forward_cos = jnp.cos(angles) * scaling[None, :]
    forward_sin = -jnp.sin(angles) * scaling[None, :]
    unscale = 1.0 / (scaling * length)
    inverse_cos = jnp.cos(angles) * unscale[:, None]
    inverse_sin = -jnp.sin(angles) * unscale[:, None]
    return forward_cos, forward_sin, inverse_cos, inverse_sin


def mode_shift(index_values, length):
    phases = index_values * (2.0 * math.pi / length)
    factor = math.exp(math.log(alpha_ratio) / length)
    return 1.0 - factor * jnp.cos(phases), factor * jnp.sin(phases)


def sweep_weights():
    return [1.0 / (1.0 + 0.4 * math.cos(math.pi * (2 * rounds + 1) / (2 * SWEEPS))) for rounds in range(SWEEPS)]


def divided(error_real, error_imag, base_part, shift_real, shift_imag):
    diag_real = shift_real + base_part
    magnitude = diag_real * diag_real + shift_imag * shift_imag
    return jnp.stack([(error_real * diag_real + error_imag * shift_imag) / magnitude,
                      (error_imag * diag_real - error_real * shift_imag) / magnitude])


def update(centre, near_sum, far_sum, target, kappa_part, base_part, shift_real, shift_imag, weight):
    applied = base_part * centre - kappa_part * (near_weight * near_sum + far_weight * far_sum)
    image_real = shift_real * centre[0] - shift_imag * centre[1] + applied[0]
    image_imag = shift_real * centre[1] + shift_imag * centre[0] + applied[1]
    error_real = target[0] - image_real
    error_imag = target[1] - image_imag
    return centre + weight * divided(error_real, error_imag, base_part, shift_real, shift_imag)


def reference(state, initial, forcing, kappa, reaction):
    kappa_full = kappa.astype(jnp.float32)
    reaction_full = reaction.astype(jnp.float32)
    start_state = initial.astype(jnp.float32)
    previous = jnp.concatenate([initial[None], state[:-1]], axis=0)

    def one_residual(item_set):
        current, earlier, source_term = item_set
        centre = current.astype(jnp.float32)
        near_sum, far_sum = cycle_sums(centre)
        result = residual_of(centre, near_sum, far_sum, earlier.astype(jnp.float32),
                             source_term.astype(jnp.float32), kappa_full, reaction_full)
        return result.astype(jnp.bfloat16)

    residual = lax.map(one_residual, (state, previous, forcing))
    forward_cos, forward_sin, inverse_cos, inverse_sin = tables(STEPS)
    flat_residual = residual.reshape(STEPS, -1).astype(jnp.float32)
    spec_real = jnp.dot(forward_cos, flat_residual, precision=highest).astype(jnp.bfloat16).reshape(state.shape)
    spec_imag = jnp.dot(forward_sin, flat_residual, precision=highest).astype(jnp.bfloat16).reshape(state.shape)
    sigma_rate = 3.0 * reaction_full * start_state * start_state
    base_rate = kappa_full * centre_weight + sigma_rate

    def one_mode(item_set):
        target_real, target_imag, mode_index = item_set
        target = jnp.stack([target_real, target_imag]).astype(jnp.float32)
        shift_real, shift_imag = mode_shift(mode_index.astype(jnp.float32), STEPS)
        iterate = divided(target[0], target[1], base_rate, shift_real, shift_imag)
        for weight in sweep_weights():
            near_sum, far_sum = cycle_sums(iterate)
            iterate = update(iterate, near_sum, far_sum, target, kappa_full, base_rate, shift_real, shift_imag, weight)
        return iterate.astype(jnp.bfloat16)

    solved = lax.map(one_mode, (spec_real, spec_imag, jnp.arange(STEPS, dtype=jnp.int32)))
    real_part = solved[:, 0].reshape(STEPS, -1).astype(jnp.float32)
    imag_part = solved[:, 1].reshape(STEPS, -1).astype(jnp.float32)
    correction = (jnp.dot(inverse_cos, real_part, precision=highest)
                  + jnp.dot(inverse_sin, imag_part, precision=highest)).astype(jnp.bfloat16).reshape(state.shape)
    return (state.astype(jnp.float32) + correction.astype(jnp.float32)).astype(jnp.bfloat16)
```

```python
import functools
import math

import jax
import jax.numpy as jnp
from jax import lax
from jax.experimental import pallas as pl
from jax.experimental.pallas import tpu as pltpu
from jax.sharding import PartitionSpec as P

SWEEPS = 6
ALPHA = 0.25
MESH = pl.DeviceIdType.MESH
f32, bf16 = jnp.float32, jnp.bfloat16
REACH = 2 * SWEEPS


def sweep_weights():
    return [1.0 / (1.0 + 0.4 * math.cos(math.pi * (2 * k + 1) / (2 * SWEEPS))) for k in range(SWEEPS)]


def pick(index, values):
    out = jnp.float32(values[0])
    for k in range(1, len(values)):
        out = jnp.where(index == k, jnp.float32(values[k]), out)
    return out


def scaled_sum(terms):
    total = None
    for factor, value in terms:
        if abs(factor) < 1e-12:
            continue
        if abs(factor - 1.0) < 1e-12:
            total = value if total is None else total + value
        elif abs(factor + 1.0) < 1e-12:
            total = -value if total is None else total - value
        else:
            part = value * jnp.float32(factor)
            total = part if total is None else total + part
    return total


def forward_transform(values):
    n = len(values)
    h = n // 2
    s = [v * jnp.float32(ALPHA ** (k / n)) if k else v for k, v in enumerate(values)]
    even = {k: s[k] + s[n - k] for k in range(1, h)}
    odd = {k: s[k] - s[n - k] for k in range(1, h)}
    even[0], even[h] = s[0], s[h]
    out = [None] * h
    ang = 2.0 * math.pi / n
    re = [None] * (h + 1)
    im = [None] * (h + 1)
    for j in range(h // 2 + 1):
        a = scaled_sum([(math.cos(ang * ((j * k) % n)), even[k]) for k in range(0, h + 1, 2)])
        b = scaled_sum([(math.cos(ang * ((j * k) % n)), even[k]) for k in range(1, h + 1, 2)])
        re[j] = a if b is None else a + b
        if h - j != j:
            re[h - j] = a if b is None else a - b
        if j:
            c = scaled_sum([(math.sin(ang * ((j * k) % n)), odd[k]) for k in range(2, h, 2)])
            d = scaled_sum([(math.sin(ang * ((j * k) % n)), odd[k]) for k in range(1, h, 2)])
            if h - j != j:
                im[j] = -(c + d)
                im[h - j] = c - d
            else:
                parts = [v for v in (c, d) if v is not None]
                im[j] = -sum(parts[1:], parts[0])
    out[0] = (re[0], re[h])
    for j in range(1, h):
        out[j] = (re[j], im[j])
    return out


def inverse_transform(pairs):
    h = len(pairs)
    n = 2 * h
    ang = 2.0 * math.pi / n
    x0, xh = pairs[0]
    re = {j: pairs[j][0] for j in range(1, h)}
    im = {j: pairs[j][1] for j in range(1, h)}
    q = h // 2
    rp = {j: re[j] + re[h - j] for j in range(1, q)}
    rm = {j: re[j] - re[h - j] for j in range(1, q)}
    ip = {j: im[j] + im[h - j] for j in range(1, q)}
    im_ = {j: im[j] - im[h - j] for j in range(1, q)}
    out = [None] * n
    s, d = x0 + xh, x0 - xh
    for k in range(h + 1):
        cos = lambda j: 2.0 * math.cos(ang * ((j * k) % n))
        sin = lambda j: 2.0 * math.sin(ang * ((j * k) % n))
        r = rp if k % 2 == 0 else rm
        i = im_ if k % 2 == 0 else ip
        c_part = scaled_sum([(cos(j), r[j]) for j in range(1, q)] + [(cos(q), re[q])])
        s_part = scaled_sum([(sin(j), i[j]) for j in range(1, q)] + [(sin(q), im[q])])
        base = s if k % 2 == 0 else d
        total = base if c_part is None else base + c_part
        scale = lambda m: jnp.float32(1.0 / (ALPHA ** (m / n) * n))
        if s_part is None:
            out[k] = total * scale(k)
            if 0 < k < h:
                out[n - k] = total * scale(n - k)
        else:
            out[k] = (total - s_part) * scale(k)
            if 0 < k < h:
                out[n - k] = (total + s_part) * scale(n - k)
    return out


def lane_sum(x, lane):
    depth = x.shape[-1]
    zero = jnp.zeros_like(x)
    near = jnp.where(lane >= 1, pltpu.roll(x, 1, 1), zero) + jnp.where(
        lane < depth - 1, pltpu.roll(x, depth - 1, 1), zero
    )
    far = jnp.where(lane >= 2, pltpu.roll(x, 2, 1), zero) + jnp.where(
        lane < depth - 2, pltpu.roll(x, depth - 2, 1), zero
    )
    return near, far


def neighbour_sum(ref, p, row, size, lane):
    c = ref[p, row : row + size, :]
    near, far = lane_sum(c, lane)
    near = near + (ref[p - 1, row : row + size, :] + ref[p + 1, row : row + size, :])
    far = far + (ref[p - 2, row : row + size, :] + ref[p + 2, row : row + size, :])
    near = near + (ref[p, row - 1 : row - 1 + size, :] + ref[p, row + 1 : row + 1 + size, :])
    far = far + (ref[p, row - 2 : row - 2 + size, :] + ref[p, row + 2 : row + 2 + size, :])
    return c, near * 0.5 + far


def kernel(
    members, slabs, width, rows,
    state, initial, forcing, kappa, reaction, out,
    prev, halo, cext, res, buf1, spec, tgt, sol, buf3, corr, buf4,
    ca, cc, ci, x0r, x0i, ar, ai, br, bi,
    prev_s, prev_r, halo_s, halo_r, coef_s, coef_r, s1, r1, s2, r2, sg, rg, s3, r3, s4, r4,
):
    chips = members // 2
    half = width // 2
    hr = half * rows
    piece = hr // chips
    ext = half + 2 * REACH
    extra = REACH - half
    depth = state.shape[1]
    me = lax.axis_index("tm")
    slab = lax.axis_index("space")
    chip = lax.div(me, 2)
    core = lax.rem(me, 2)
    part = slab * 2 + core
    parts = 2 * slabs
    chunks = [(r, 16) for r in range(0, rows, 16)]

    barrier = pltpu.get_barrier_semaphore()

    def greet(k, _):
        other = lax.rem(me + k, members)
        pl.semaphore_signal(barrier, inc=1, device_id=(other, slab), device_id_type=MESH)
        return 0

    lax.fori_loop(1, members, greet, 0)
    has_low = slab > 0
    has_high = slab < slabs - 1
    for flag, step in ((has_low, -1), (has_high, 1)):
        @pl.when(flag)
        def _():
            for c in range(2):
                pl.semaphore_signal(
                    barrier, inc=1, device_id=(chip * 2 + c, slab + step), device_id_type=MESH
                )
    pl.semaphore_wait(
        barrier,
        members - 1 + 2 * has_low.astype(jnp.int32) + 2 * has_high.astype(jnp.int32),
    )

    def remote(src, dst, send, recv, device):
        return pltpu.make_async_remote_copy(
            src_ref=src, dst_ref=dst, send_sem=send, recv_sem=recv,
            device_id=device, device_id_type=MESH,
        )

    def prev_copy():
        return remote(state, prev, prev_s, prev_r, (lax.rem(me + 1, members), slab))

    @pl.when(me < members - 1)
    def _():
        prev_copy().start()

    def halo_copy(side):
        src = state.at[pl.ds((width - 2) * rows, 2 * rows), :] if side == 0 else state.at[pl.ds(0, 2 * rows), :]
        return remote(src, halo.at[side], halo_s.at[side], halo_r.at[side],
                      (me, slab + (1 if side == 0 else -1)))

    sends = (has_high, has_low)
    gets = (has_low, has_high)
    for side in range(2):
        @pl.when(sends[side])
        def _():
            halo_copy(side).start()

        @pl.when(jnp.logical_not(gets[side]))
        def _():
            halo[side] = jnp.zeros((2 * rows, depth), bf16)

    moves = (
        (1, 0, half, REACH - half),
        (-1, 0, half, REACH + half),
        (2, half - extra, extra, 0),
        (-2, 0, extra, REACH + 2 * half),
    )

    def there(step):
        return jnp.logical_and(part + step >= 0, part + step < parts)

    def device_at(step):
        target = part + step
        return (chip * 2 + lax.rem(target + 2, 2), lax.div(target + 2, 2) - 1)

    coefs = (kappa, reaction, initial)

    def coef_copy(m, a):
        step, first, count, place = moves[m]
        src = coefs[a].at[pl.ds(pl.multiple_of(core * hr + first * rows, 16), count * rows), :]
        return remote(src, cext.at[a, pl.ds(place * rows, count * rows), :],
                      coef_s.at[m, a], coef_r.at[m, a], device_at(step))

    def target_copy(m):
        step, first, count, place = moves[m]
        return remote(tgt.at[:, pl.ds((REACH + first) * rows, count * rows), :],
                      tgt.at[:, pl.ds(place * rows, count * rows), :],
                      sg.at[m], rg.at[m], device_at(step))

    for m, (step, first, count, place) in enumerate(moves):
        @pl.when(there(step))
        def _():
            for a in range(3):
                coef_copy(m, a).start()

        @pl.when(jnp.logical_not(there(-step)))
        def _():
            for a in range(3):
                cext[a, pl.ds(place * rows, count * rows), :] = jnp.zeros((count * rows, depth), bf16)
            for a in range(2):
                tgt[a, pl.ds(place * rows, count * rows), :] = jnp.zeros((count * rows, depth), bf16)

    for a in range(3):
        cext[a, pl.ds(REACH * rows, hr), :] = coefs[a][pl.ds(pl.multiple_of(core * hr, 16), hr), :]

    pad = jnp.zeros((8, depth), f32)

    def clear(p, _):
        for ref in (ar, ai, br, bi):
            ref[p, 0:8, :] = pad
            ref[p, 8 + rows : 16 + rows, :] = pad
        return 0

    lax.fori_loop(0, ext, clear, 0)
    lane = lax.broadcasted_iota(jnp.int32, (16, depth), 1)

    def widen(p, _):
        for r, n in chunks:
            at = pl.ds(pl.multiple_of(p * rows, 16) + r, n)
            ar[p + 2, 8 + r : 8 + r + n, :] = state[at, :].astype(f32)
        return 0

    lax.fori_loop(0, width, widen, 0)
    for side in range(2):
        @pl.when(gets[side])
        def _():
            halo_copy(side).wait_recv()
        for p in range(2):
            at = p if side == 0 else width + 2 + p
            ar[at, 8 : 8 + rows, :] = halo[side, p * rows : (p + 1) * rows, :].astype(f32)

    @pl.when(me == 0)
    def _():
        prev[...] = initial[...]

    @pl.when(me > 0)
    def _():
        prev_copy().wait_recv()

    def piece_copy(i):
        owner = 2 * lax.rem(i, chips) + lax.div(i, chips)
        return owner, remote(res.at[pl.ds(pl.multiple_of(i * piece, 16), piece), :], buf1.at[me],
                             s1.at[i], r1.at[me], (owner, slab))

    per_plane = rows // piece

    def residual_plane(k, _):
        p = lax.rem(k + core * half + lax.div(chip, per_plane) + 1, width)
        for r, n in chunks:
            at = pl.ds(pl.multiple_of(p * rows, 16) + r, n)
            c, total = neighbour_sum(ar, p + 2, 8 + r, n, lane)
            kap = kappa[at, :].astype(f32)
            value = (
                forcing[at, :].astype(f32) - c + prev[at, :].astype(f32)
                - kap * (9.0 * c - total)
                - reaction[at, :].astype(f32) * c * c * c
            )
            res[at, :] = value.astype(bf16)
        for sub in range(per_plane):
            i = p * per_plane + sub
            owner, copy = piece_copy(i)

            @pl.when(owner != me)
            def _():
                copy.start()
        return 0

    lax.fori_loop(0, width, residual_plane, 0)
    mine = core * chips + chip
    buf1[me] = res[pl.ds(pl.multiple_of(mine * piece, 16), piece), :]

    for m, (step, first, count, place) in enumerate(moves):
        @pl.when(there(-step))
        def _():
            for a in range(3):
                coef_copy(m, a).wait_recv()

    b = ALPHA ** (1.0 / members)
    ang = 2.0 * math.pi / members
    shift_a = pick(chip, [1.0 - b * math.cos(ang * j) for j in range(chips)])
    shift_c = pick(chip, [1.0 + b] + [1.0 - b * math.cos(ang * j) for j in range(1, chips)])
    shift_i = pick(chip, [0.0] + [b * math.sin(ang * j) for j in range(1, chips)])

    def coefficients(p, _):
        for r, n in chunks:
            at = pl.ds(pl.multiple_of(p * rows, 16) + r, n)
            kap = cext[0, at, :].astype(f32)
            ini = cext[2, at, :].astype(f32)
            base = 9.0 * kap + 3.0 * cext[1, at, :].astype(f32) * ini * ini
            da = shift_a + base
            dc = shift_c + base
            ia = 1.0 / (da * da + shift_i * shift_i)
            ic = 1.0 / (dc * dc + shift_i * shift_i)
            ca[at, :] = da * ia
            cc[at, :] = dc * ic
            ci[at, :] = shift_i * ia
        return 0

    lax.fori_loop(0, ext, coefficients, 0)

    def wait_1(n, _):
        @pl.when(n != me)
        def _():
            remote(res.at[pl.ds(0, piece), :], buf1.at[n], s1.at[0], r1.at[n], (me, slab)).wait_recv()
        return 0

    lax.fori_loop(0, members, wait_1, 0)

    def transform(t, _):
        at = pl.ds(pl.multiple_of(t * 16, 16), 16)
        pairs = forward_transform([buf1[n, at, :].astype(f32) for n in range(members)])
        for j in range(chips):
            spec[j, 0, at, :] = pairs[j][0].astype(bf16)
            spec[j, 1, at, :] = pairs[j][1].astype(bf16)
        return 0

    lax.fori_loop(0, piece // 16, transform, 0)

    def my_rows(first):
        return pl.ds(pl.multiple_of(first * rows + chip * piece, 16), piece)

    def spec_copy(j):
        return remote(spec.at[j], tgt.at[:, my_rows(REACH), :], s2.at[j], r2.at[chip],
                      (2 * j + core, slab))

    def send_2(k, _):
        spec_copy(lax.rem(chip + k, chips)).start()
        return 0

    lax.fori_loop(1, chips, send_2, 0)
    tgt[:, my_rows(REACH), :] = spec[chip]

    def wait_2(k, _):
        j = lax.rem(chip + k, chips)
        remote(spec.at[0], tgt.at[:, pl.ds(pl.multiple_of(REACH * rows + j * piece, 16), piece), :],
               s2.at[0], r2.at[j], (me, slab)).wait_recv()
        return 0

    lax.fori_loop(1, chips, wait_2, 0)
    for m, (step, first, count, place) in enumerate(moves):
        @pl.when(there(step))
        def _():
            target_copy(m).start()

    def opening(p, _):
        for r, n in chunks:
            at = pl.ds(pl.multiple_of(p * rows, 16) + r, n)
            yr = tgt[0, at, :].astype(f32)
            yi = tgt[1, at, :].astype(f32)
            kap = cext[0, at, :].astype(f32)
            a, c, i = ca[at, :], cc[at, :], ci[at, :]
            xr = yr * a + yi * i
            xi = yi * c - yr * i
            x0r[at, :] = xr
            x0i[at, :] = xi
            ar[p, 8 + r : 8 + r + n, :] = xr
            ai[p, 8 + r : 8 + r + n, :] = xi
            ca[at, :] = a * kap
            cc[at, :] = c * kap
            ci[at, :] = i * kap
        return 0

    lax.fori_loop(REACH, REACH + half, opening, 0)
    for m, (step, first, count, place) in enumerate(moves):
        @pl.when(there(-step))
        def _():
            target_copy(m).wait_recv()
    lax.fori_loop(0, REACH, opening, 0)
    lax.fori_loop(REACH + half, ext, opening, 0)

    weights = sweep_weights()
    for k in range(SWEEPS):
        sr, si, dr, di = (ar, ai, br, bi) if k % 2 == 0 else (br, bi, ar, ai)
        w = weights[k]
        last = k == SWEEPS - 1

        def sweep(p, _):
            for r, n in chunks:
                at = pl.ds(pl.multiple_of(p * rows, 16) + r, n)
                xr, tr = neighbour_sum(sr, p, 8 + r, n, lane)
                xi, ti = neighbour_sum(si, p, 8 + r, n, lane)
                i = ci[at, :]
                nr = (x0r[at, :] + ca[at, :] * tr + i * ti) * w + xr * (1.0 - w)
                ni = (x0i[at, :] + cc[at, :] * ti - i * tr) * w + xi * (1.0 - w)
                if last:
                    to = pl.ds(pl.multiple_of((p - REACH) * rows, 16) + r, n)
                    sol[0, to, :] = nr.astype(bf16)
                    sol[1, to, :] = ni.astype(bf16)
                else:
                    dr[p, 8 + r : 8 + r + n, :] = nr
                    di[p, 8 + r : 8 + r + n, :] = ni
            return 0

        lax.fori_loop(2 * k + 2, ext - 2 * k - 2, sweep, 0)

    def send_3(k, _):
        j = lax.rem(chip + k, chips)
        remote(sol.at[:, pl.ds(pl.multiple_of(j * piece, 16), piece), :], buf3.at[chip],
               s3.at[j], r3.at[chip], (2 * j + core, slab)).start()
        return 0

    lax.fori_loop(1, chips, send_3, 0)
    buf3[chip] = sol[:, my_rows(0), :]

    def wait_3(k, _):
        j = lax.rem(chip + k, chips)
        remote(sol.at[:, pl.ds(0, piece), :], buf3.at[j], s3.at[0], r3.at[j], (me, slab)).wait_recv()
        return 0

    lax.fori_loop(1, chips, wait_3, 0)

    def back(t, _):
        at = pl.ds(pl.multiple_of(t * 16, 16), 16)
        pairs = [(buf3[j, 0, at, :].astype(f32), buf3[j, 1, at, :].astype(f32)) for j in range(chips)]
        for n, value in enumerate(inverse_transform(pairs)):
            corr[n, at, :] = value.astype(bf16)
        return 0

    lax.fori_loop(0, piece // 16, back, 0)
    here = pl.ds(pl.multiple_of(mine * piece, 16), piece)

    def send_4(k, _):
        n = lax.rem(me + k, members)
        remote(corr.at[n], buf4.at[here, :], s4.at[n], r4.at[mine], (n, slab)).start()
        return 0

    lax.fori_loop(1, members, send_4, 0)
    buf4[here, :] = corr[me]

    def wait_4(i, _):
        @pl.when(i != mine)
        def _():
            remote(corr.at[0], buf4.at[pl.ds(pl.multiple_of(i * piece, 16), piece), :],
                   s4.at[0], r4.at[i], (me, slab)).wait_recv()
        return 0

    lax.fori_loop(0, members, wait_4, 0)

    def finish(p, _):
        for r, n in chunks:
            at = pl.ds(pl.multiple_of(p * rows, 16) + r, n)
            out[at, :] = (state[at, :].astype(f32) + buf4[at, :].astype(f32)).astype(bf16)
        return 0

    lax.fori_loop(0, width, finish, 0)

    @pl.when(me < members - 1)
    def _():
        prev_copy().wait_send()

    for side in range(2):
        @pl.when(sends[side])
        def _():
            halo_copy(side).wait_send()
    for m, (step, first, count, place) in enumerate(moves):
        @pl.when(there(step))
        def _():
            for a in range(3):
                coef_copy(m, a).wait_send()
            target_copy(m).wait_send()

    def drain_members(n, _):
        owner, copy = piece_copy(n)

        @pl.when(owner != me)
        def _():
            copy.wait_send()

        @pl.when(n != me)
        def _():
            remote(corr.at[n], buf4.at[here, :], s4.at[n], r4.at[mine], (n, slab)).wait_send()
        return 0

    lax.fori_loop(0, members, drain_members, 0)

    def drain_chips(k, _):
        j = lax.rem(chip + k, chips)
        spec_copy(j).wait_send()
        remote(sol.at[:, pl.ds(pl.multiple_of(j * piece, 16), piece), :], buf3.at[chip],
               s3.at[j], r3.at[chip], (2 * j + core, slab)).wait_send()
        return 0

    lax.fori_loop(1, chips, drain_chips, 0)


def on_device(state, initial, forcing, kappa, reaction):
    steps, width, rows, depth = state.shape
    assert steps == 1
    members = lax.axis_size("tm")
    slabs = lax.axis_size("space")
    chips = members // 2
    half = width // 2
    total = width * rows
    piece = half * rows // chips
    ext = half + 2 * REACH
    dma = pltpu.SemaphoreType.DMA
    flat = lambda a: a.reshape(total, depth)
    padded = pltpu.VMEM((ext, rows + 16, depth), f32)
    wide = pltpu.VMEM((ext * rows, depth), f32)
    out = pl.pallas_call(
        functools.partial(kernel, members, slabs, width, rows),
        out_shape=jax.ShapeDtypeStruct((total, depth), bf16),
        in_specs=[pl.BlockSpec(memory_space=pltpu.VMEM)] * 5,
        out_specs=pl.BlockSpec(memory_space=pltpu.VMEM),
        scratch_shapes=[
            pltpu.VMEM((total, depth), bf16),
            pltpu.VMEM((2, 2 * rows, depth), bf16),
            pltpu.VMEM((3, ext * rows, depth), bf16),
            pltpu.VMEM((total, depth), bf16),
            pltpu.VMEM((members, piece, depth), bf16),
            pltpu.VMEM((chips, 2, piece, depth), bf16),
            pltpu.VMEM((2, ext * rows, depth), bf16),
            pltpu.VMEM((2, half * rows, depth), bf16),
            pltpu.VMEM((chips, 2, piece, depth), bf16),
            pltpu.VMEM((members, piece, depth), bf16),
            pltpu.VMEM((total, depth), bf16),
            wide, wide, wide, wide, wide,
            padded, padded, padded, padded,
            dma, dma, dma((2,)), dma((2,)), dma((4, 3)), dma((4, 3)),
            dma((members,)), dma((members,)), dma((chips,)), dma((chips,)),
            dma((4,)), dma((4,)), dma((chips,)), dma((chips,)), dma((members,)), dma((members,)),
        ],
        compiler_params=pltpu.CompilerParams(
            collective_id=0, has_side_effects=True, vmem_limit_bytes=40 * 2**20
        ),
    )(flat(state), flat(initial), flat(forcing), flat(kappa), flat(reaction))
    return out.reshape(state.shape)


def solution(mesh):
    cells = P("space", None, None)
    return jax.shard_map(
        on_device,
        mesh=mesh,
        in_specs=(P("tm", "space", None, None), cells, P("tm", "space", None, None), cells, cells),
        out_specs=P("tm", "space", None, None),
        check_vma=False,
    )
```

```python
import functools
import math

import jax
import jax.numpy as jnp
from jax import lax
from jax.experimental import pallas as pl
from jax.experimental.pallas import tpu as pltpu
from jax.sharding import PartitionSpec as P

SWEEPS = 6
ALPHA = 0.25
MESH = pl.DeviceIdType.MESH
f32, bf16 = jnp.float32, jnp.bfloat16
REACH = 2 * SWEEPS


def sweep_weights():
    return [1.0 / (1.0 + 0.4 * math.cos(math.pi * (2 * k + 1) / (2 * SWEEPS))) for k in range(SWEEPS)]


def pick(index, values):
    out = jnp.float32(values[0])
    for k in range(1, len(values)):
        out = jnp.where(index == k, jnp.float32(values[k]), out)
    return out


def scaled_sum(terms):
    total = None
    for factor, value in terms:
        if abs(factor) < 1e-12:
            continue
        if abs(factor - 1.0) < 1e-12:
            total = value if total is None else total + value
        elif abs(factor + 1.0) < 1e-12:
            total = -value if total is None else total - value
        else:
            part = value * jnp.float32(factor)
            total = part if total is None else total + part
    return total


def forward_transform(values):
    n = len(values)
    h = n // 2
    s = [v * jnp.float32(ALPHA ** (k / n)) if k else v for k, v in enumerate(values)]
    even = {k: s[k] + s[n - k] for k in range(1, h)}
    odd = {k: s[k] - s[n - k] for k in range(1, h)}
    even[0], even[h] = s[0], s[h]
    out = [None] * h
    ang = 2.0 * math.pi / n
    re = [None] * (h + 1)
    im = [None] * (h + 1)
    for j in range(h // 2 + 1):
        a = scaled_sum([(math.cos(ang * ((j * k) % n)), even[k]) for k in range(0, h + 1, 2)])
        b = scaled_sum([(math.cos(ang * ((j * k) % n)), even[k]) for k in range(1, h + 1, 2)])
        re[j] = a if b is None else a + b
        if h - j != j:
            re[h - j] = a if b is None else a - b
        if j:
            c = scaled_sum([(math.sin(ang * ((j * k) % n)), odd[k]) for k in range(2, h, 2)])
            d = scaled_sum([(math.sin(ang * ((j * k) % n)), odd[k]) for k in range(1, h, 2)])
            if h - j != j:
                im[j] = -(c + d)
                im[h - j] = c - d
            else:
                parts = [v for v in (c, d) if v is not None]
                im[j] = -sum(parts[1:], parts[0])
    out[0] = (re[0], re[h])
    for j in range(1, h):
        out[j] = (re[j], im[j])
    return out


def inverse_transform(pairs):
    h = len(pairs)
    n = 2 * h
    ang = 2.0 * math.pi / n
    x0, xh = pairs[0]
    re = {j: pairs[j][0] for j in range(1, h)}
    im = {j: pairs[j][1] for j in range(1, h)}
    q = h // 2
    rp = {j: re[j] + re[h - j] for j in range(1, q)}
    rm = {j: re[j] - re[h - j] for j in range(1, q)}
    ip = {j: im[j] + im[h - j] for j in range(1, q)}
    im_ = {j: im[j] - im[h - j] for j in range(1, q)}
    out = [None] * n
    s, d = x0 + xh, x0 - xh
    for k in range(h + 1):
        cos = lambda j: 2.0 * math.cos(ang * ((j * k) % n))
        sin = lambda j: 2.0 * math.sin(ang * ((j * k) % n))
        r = rp if k % 2 == 0 else rm
        i = im_ if k % 2 == 0 else ip
        c_part = scaled_sum([(cos(j), r[j]) for j in range(1, q)] + [(cos(q), re[q])])
        s_part = scaled_sum([(sin(j), i[j]) for j in range(1, q)] + [(sin(q), im[q])])
        base = s if k % 2 == 0 else d
        total = base if c_part is None else base + c_part
        scale = lambda m: jnp.float32(1.0 / (ALPHA ** (m / n) * n))
        if s_part is None:
            out[k] = total * scale(k)
            if 0 < k < h:
                out[n - k] = total * scale(n - k)
        else:
            out[k] = (total - s_part) * scale(k)
            if 0 < k < h:
                out[n - k] = (total + s_part) * scale(n - k)
    return out


def lane_sum(x, lane):
    depth = x.shape[-1]
    zero = jnp.zeros_like(x)
    near = jnp.where(lane >= 1, pltpu.roll(x, 1, 1), zero) + jnp.where(
        lane < depth - 1, pltpu.roll(x, depth - 1, 1), zero
    )
    far = jnp.where(lane >= 2, pltpu.roll(x, 2, 1), zero) + jnp.where(
        lane < depth - 2, pltpu.roll(x, depth - 2, 1), zero
    )
    return near, far


def neighbour_sum(ref, p, row, size, lane):
    c = ref[p, row : row + size, :]
    near, far = lane_sum(c, lane)
    near = near + (ref[p - 1, row : row + size, :] + ref[p + 1, row : row + size, :])
    far = far + (ref[p - 2, row : row + size, :] + ref[p + 2, row : row + size, :])
    near = near + (ref[p, row - 1 : row - 1 + size, :] + ref[p, row + 1 : row + 1 + size, :])
    far = far + (ref[p, row - 2 : row - 2 + size, :] + ref[p, row + 2 : row + 2 + size, :])
    return c, near * 0.5 + far


def kernel(
    members, slabs, width, rows,
    state_h, initial_h, forcing_h, kappa_h, reaction_h, out,
    state, initial, forcing, kappa, reaction, load_s,
    prev, halo, cext, res, buf1, spec, tgt, sol, buf3, corr, buf4,
    ca, cc, ci, x0r, x0i, ar, ai, br, bi,
    prev_s, prev_r, halo_s, halo_r, coef_s, coef_r, s1, r1, s2, r2, sg, rg, s3, r3, s4, r4,
):
    chips = members // 2
    half = width // 2
    hr = half * rows
    piece = hr // chips
    ext = half + 2 * REACH
    extra = REACH - half
    depth = state.shape[1]
    me = lax.axis_index("tm")
    slab = lax.axis_index("space")
    chip = lax.div(me, 2)
    core = lax.rem(me, 2)
    part = slab * 2 + core
    parts = 2 * slabs
    chunks = [(r, 16) for r in range(0, rows, 16)]

    loads = [
        pltpu.make_async_copy(src, dst, load_s.at[k])
        for k, (src, dst) in enumerate((
            (state_h, state), (kappa_h, kappa), (reaction_h, reaction),
            (initial_h, initial), (forcing_h, forcing),
        ))
    ]
    for load in loads:
        load.start()

    barrier = pltpu.get_barrier_semaphore()

    def greet(k, _):
        other = lax.rem(me + k, members)
        pl.semaphore_signal(barrier, inc=1, device_id=(other, slab), device_id_type=MESH)
        return 0

    lax.fori_loop(1, members, greet, 0)
    has_low = slab > 0
    has_high = slab < slabs - 1
    for flag, step in ((has_low, -1), (has_high, 1)):
        @pl.when(flag)
        def _():
            for c in range(2):
                pl.semaphore_signal(
                    barrier, inc=1, device_id=(chip * 2 + c, slab + step), device_id_type=MESH
                )
    pad = jnp.zeros((8, depth), f32)

    def clear(p, _):
        for ref in (ar, ai, br, bi):
            ref[p, 0:8, :] = pad
            ref[p, 8 + rows : 16 + rows, :] = pad
        return 0

    lax.fori_loop(0, ext, clear, 0)
    pl.semaphore_wait(
        barrier,
        members - 1 + 2 * has_low.astype(jnp.int32) + 2 * has_high.astype(jnp.int32),
    )

    def remote(src, dst, send, recv, device):
        return pltpu.make_async_remote_copy(
            src_ref=src, dst_ref=dst, send_sem=send, recv_sem=recv,
            device_id=device, device_id_type=MESH,
        )

    def prev_copy():
        return remote(state, prev, prev_s, prev_r, (lax.rem(me + 1, members), slab))

    loads[0].wait()

    @pl.when(me < members - 1)
    def _():
        prev_copy().start()

    def halo_copy(side):
        src = state.at[pl.ds((width - 2) * rows, 2 * rows), :] if side == 0 else state.at[pl.ds(0, 2 * rows), :]
        return remote(src, halo.at[side], halo_s.at[side], halo_r.at[side],
                      (me, slab + (1 if side == 0 else -1)))

    sends = (has_high, has_low)
    gets = (has_low, has_high)
    for side in range(2):
        @pl.when(sends[side])
        def _():
            halo_copy(side).start()

        @pl.when(jnp.logical_not(gets[side]))
        def _():
            halo[side] = jnp.zeros((2 * rows, depth), bf16)

    moves = (
        (1, 0, half, REACH - half),
        (-1, 0, half, REACH + half),
        (2, half - extra, extra, 0),
        (-2, 0, extra, REACH + 2 * half),
    )

    def there(step):
        return jnp.logical_and(part + step >= 0, part + step < parts)

    def device_at(step):
        target = part + step
        return (chip * 2 + lax.rem(target + 2, 2), lax.div(target + 2, 2) - 1)

    coefs = (kappa, reaction, initial)

    def coef_copy(m, a):
        step, first, count, place = moves[m]
        src = coefs[a].at[pl.ds(pl.multiple_of(core * hr + first * rows, 16), count * rows), :]
        return remote(src, cext.at[a, pl.ds(place * rows, count * rows), :],
                      coef_s.at[m, a], coef_r.at[m, a], device_at(step))

    for load in loads[1:4]:
        load.wait()
    for m, (step, first, count, place) in enumerate(moves):
        @pl.when(there(step))
        def _():
            for a in range(3):
                coef_copy(m, a).start()

        @pl.when(jnp.logical_not(there(-step)))
        def _():
            for a in range(3):
                cext[a, pl.ds(place * rows, count * rows), :] = jnp.zeros((count * rows, depth), bf16)
            for a in range(2):
                tgt[a, pl.ds(place * rows, count * rows), :] = jnp.zeros((count * rows, depth), bf16)

    for a in range(3):
        cext[a, pl.ds(REACH * rows, hr), :] = coefs[a][pl.ds(pl.multiple_of(core * hr, 16), hr), :]

    lane = lax.broadcasted_iota(jnp.int32, (16, depth), 1)

    def widen(p, _):
        for r, n in chunks:
            at = pl.ds(pl.multiple_of(p * rows, 16) + r, n)
            ar[p + 2, 8 + r : 8 + r + n, :] = state[at, :].astype(f32)
        return 0

    lax.fori_loop(0, width, widen, 0)
    for side in range(2):
        @pl.when(gets[side])
        def _():
            halo_copy(side).wait_recv()
        for p in range(2):
            at = p if side == 0 else width + 2 + p
            ar[at, 8 : 8 + rows, :] = halo[side, p * rows : (p + 1) * rows, :].astype(f32)

    loads[4].wait()

    @pl.when(me == 0)
    def _():
        prev[...] = initial[...]

    @pl.when(me > 0)
    def _():
        prev_copy().wait_recv()

    def piece_copy(i):
        owner = 2 * lax.rem(i, chips) + lax.div(i, chips)
        return owner, remote(res.at[pl.ds(pl.multiple_of(i * piece, 16), piece), :], buf1.at[me],
                             s1.at[i], r1.at[me], (owner, slab))

    per_plane = rows // piece

    def residual_plane(k, _):
        p = lax.rem(k + core * half + lax.div(chip, per_plane) + 1, width)
        for r, n in chunks:
            at = pl.ds(pl.multiple_of(p * rows, 16) + r, n)
            c, total = neighbour_sum(ar, p + 2, 8 + r, n, lane)
            kap = kappa[at, :].astype(f32)
            value = (
                forcing[at, :].astype(f32) - c + prev[at, :].astype(f32)
                - kap * (9.0 * c - total)
                - reaction[at, :].astype(f32) * c * c * c
            )
            res[at, :] = value.astype(bf16)
        for sub in range(per_plane):
            i = p * per_plane + sub
            owner, copy = piece_copy(i)

            @pl.when(owner != me)
            def _():
                copy.start()
        return 0

    lax.fori_loop(0, width, residual_plane, 0)
    mine = core * chips + chip
    buf1[me] = res[pl.ds(pl.multiple_of(mine * piece, 16), piece), :]

    def wait_1(n, _):
        @pl.when(n != me)
        def _():
            remote(res.at[pl.ds(0, piece), :], buf1.at[n], s1.at[0], r1.at[n], (me, slab)).wait_recv()
        return 0

    lax.fori_loop(0, members, wait_1, 0)

    def transform(t, _):
        at = pl.ds(pl.multiple_of(t * 16, 16), 16)
        pairs = forward_transform([buf1[n, at, :].astype(f32) for n in range(members)])
        for j in range(chips):
            spec[j, 0, at, :] = pairs[j][0].astype(bf16)
            spec[j, 1, at, :] = pairs[j][1].astype(bf16)
        return 0

    lax.fori_loop(0, piece // 16, transform, 0)

    def my_rows(first):
        return pl.ds(pl.multiple_of(first * rows + chip * piece, 16), piece)

    def spec_copy(j):
        return remote(spec.at[j], tgt.at[:, my_rows(REACH), :], s2.at[j], r2.at[chip],
                      (2 * j + core, slab))

    def send_2(k, _):
        spec_copy(lax.rem(chip + k, chips)).start()
        return 0

    lax.fori_loop(1, chips, send_2, 0)
    tgt[:, my_rows(REACH), :] = spec[chip]

    def forward(j, action):
        at = j * piece
        for m, (step, first, count, place) in enumerate(moves):
            inside = jnp.logical_and(at >= first * rows, at < (first + count) * rows)

            @pl.when(jnp.logical_and(there(step), inside))
            def _():
                target = pl.multiple_of(place * rows + at - first * rows, 16)
                copy = remote(
                    tgt.at[:, pl.ds(pl.multiple_of(REACH * rows + at, 16), piece), :],
                    tgt.at[:, pl.ds(target, piece), :],
                    sg.at[m, j], rg.at[m, j], device_at(step))
                action(copy)

    def arrived(m, j):
        step, first, count, place = moves[m]
        at = j * piece
        inside = jnp.logical_and(at >= first * rows, at < (first + count) * rows)

        @pl.when(jnp.logical_and(there(-step), inside))
        def _():
            target = pl.multiple_of(place * rows + at - first * rows, 16)
            remote(
                tgt.at[:, pl.ds(REACH * rows, piece), :],
                tgt.at[:, pl.ds(target, piece), :],
                sg.at[m, j], rg.at[m, j], (me, slab)).wait_recv()

    forward(chip, lambda copy: copy.start())

    def wait_2(k, _):
        j = lax.rem(chip + chips - k, chips)
        remote(spec.at[0], tgt.at[:, pl.ds(pl.multiple_of(REACH * rows + j * piece, 16), piece), :],
               s2.at[0], r2.at[j], (me, slab)).wait_recv()
        forward(j, lambda copy: copy.start())
        return 0

    lax.fori_loop(1, chips, wait_2, 0)

    for m, (step, first, count, place) in enumerate(moves):
        @pl.when(there(-step))
        def _():
            for a in range(3):
                coef_copy(m, a).wait_recv()

    b = ALPHA ** (1.0 / members)
    ang = 2.0 * math.pi / members
    shift_a = pick(chip, [1.0 - b * math.cos(ang * j) for j in range(chips)])
    shift_c = pick(chip, [1.0 + b] + [1.0 - b * math.cos(ang * j) for j in range(1, chips)])
    shift_i = pick(chip, [0.0] + [b * math.sin(ang * j) for j in range(1, chips)])

    def coefficients(p, _):
        for r, n in chunks:
            at = pl.ds(pl.multiple_of(p * rows, 16) + r, n)
            kap = cext[0, at, :].astype(f32)
            ini = cext[2, at, :].astype(f32)
            base = 9.0 * kap + 3.0 * cext[1, at, :].astype(f32) * ini * ini
            da = shift_a + base
            dc = shift_c + base
            ia = 1.0 / (da * da + shift_i * shift_i)
            ic = 1.0 / (dc * dc + shift_i * shift_i)
            ca[at, :] = da * ia
            cc[at, :] = dc * ic
            ci[at, :] = shift_i * ia
        return 0

    lax.fori_loop(0, ext, coefficients, 0)

    def opening(p, _):
        for r, n in chunks:
            at = pl.ds(pl.multiple_of(p * rows, 16) + r, n)
            yr = tgt[0, at, :].astype(f32)
            yi = tgt[1, at, :].astype(f32)
            kap = cext[0, at, :].astype(f32)
            a, c, i = ca[at, :], cc[at, :], ci[at, :]
            xr = yr * a + yi * i
            xi = yi * c - yr * i
            x0r[at, :] = xr
            x0i[at, :] = xi
            ar[p, 8 + r : 8 + r + n, :] = xr
            ai[p, 8 + r : 8 + r + n, :] = xi
            ca[at, :] = a * kap
            cc[at, :] = c * kap
            ci[at, :] = i * kap
        return 0

    lax.fori_loop(REACH, REACH + half, opening, 0)
    def arrivals(k, _):
        j = lax.rem(chip + chips - k, chips)
        for m in range(4):
            arrived(m, j)
        return 0

    lax.fori_loop(0, chips, arrivals, 0)
    lax.fori_loop(0, REACH, opening, 0)
    lax.fori_loop(REACH + half, ext, opening, 0)

    def solved_copy(j):
        return remote(sol.at[:, pl.ds(pl.multiple_of(j * piece, 16), piece), :], buf3.at[chip],
                      s3.at[j], r3.at[chip], (2 * j + core, slab))

    weights = sweep_weights()
    for k in range(SWEEPS):
        sr, si, dr, di = (ar, ai, br, bi) if k % 2 == 0 else (br, bi, ar, ai)
        w = weights[k]
        last = k == SWEEPS - 1

        def sweep(turn, _):
            p = turn
            if last:
                plane = lax.rem(turn - REACH + lax.div(chip, per_plane) + 1, half)
                p = plane + REACH
            for r, n in chunks:
                at = pl.ds(pl.multiple_of(p * rows, 16) + r, n)
                xr, tr = neighbour_sum(sr, p, 8 + r, n, lane)
                xi, ti = neighbour_sum(si, p, 8 + r, n, lane)
                i = ci[at, :]
                nr = (x0r[at, :] + ca[at, :] * tr + i * ti) * w + xr * (1.0 - w)
                ni = (x0i[at, :] + cc[at, :] * ti - i * tr) * w + xi * (1.0 - w)
                if last:
                    to = pl.ds(pl.multiple_of((p - REACH) * rows, 16) + r, n)
                    sol[0, to, :] = nr.astype(bf16)
                    sol[1, to, :] = ni.astype(bf16)
                else:
                    dr[p, 8 + r : 8 + r + n, :] = nr
                    di[p, 8 + r : 8 + r + n, :] = ni
            if last:
                for sub in range(per_plane):
                    j = plane * per_plane + sub

                    @pl.when(j != chip)
                    def _():
                        solved_copy(j).start()
            return 0

        lax.fori_loop(2 * k + 2, ext - 2 * k - 2, sweep, 0)

    buf3[chip] = sol[:, my_rows(0), :]

    def wait_3(k, _):
        j = lax.rem(chip + k, chips)
        remote(sol.at[:, pl.ds(0, piece), :], buf3.at[j], s3.at[0], r3.at[j], (me, slab)).wait_recv()
        return 0

    lax.fori_loop(1, chips, wait_3, 0)

    def back(t, _):
        at = pl.ds(pl.multiple_of(t * 16, 16), 16)
        pairs = [(buf3[j, 0, at, :].astype(f32), buf3[j, 1, at, :].astype(f32)) for j in range(chips)]
        for n, value in enumerate(inverse_transform(pairs)):
            corr[n, at, :] = value.astype(bf16)
        return 0

    lax.fori_loop(0, piece // 16, back, 0)
    here = pl.ds(pl.multiple_of(mine * piece, 16), piece)

    def send_4(k, _):
        n = lax.rem(me + k, members)
        remote(corr.at[n], buf4.at[here, :], s4.at[n], r4.at[mine], (n, slab)).start()
        return 0

    lax.fori_loop(1, members, send_4, 0)
    buf4[here, :] = corr[me]

    def wait_4(i, _):
        @pl.when(i != mine)
        def _():
            remote(corr.at[0], buf4.at[pl.ds(pl.multiple_of(i * piece, 16), piece), :],
                   s4.at[0], r4.at[i], (me, slab)).wait_recv()
        return 0

    lax.fori_loop(0, members, wait_4, 0)

    def finish(p, _):
        for r, n in chunks:
            at = pl.ds(pl.multiple_of(p * rows, 16) + r, n)
            out[at, :] = (state[at, :].astype(f32) + buf4[at, :].astype(f32)).astype(bf16)
        return 0

    lax.fori_loop(0, width, finish, 0)

    @pl.when(me < members - 1)
    def _():
        prev_copy().wait_send()

    for side in range(2):
        @pl.when(sends[side])
        def _():
            halo_copy(side).wait_send()
    for m, (step, first, count, place) in enumerate(moves):
        @pl.when(there(step))
        def _():
            for a in range(3):
                coef_copy(m, a).wait_send()

    def drain_members(n, _):
        owner, copy = piece_copy(n)

        @pl.when(owner != me)
        def _():
            copy.wait_send()

        @pl.when(n != me)
        def _():
            remote(corr.at[n], buf4.at[here, :], s4.at[n], r4.at[mine], (n, slab)).wait_send()
        return 0

    lax.fori_loop(0, members, drain_members, 0)

    def drain_chips(k, _):
        j = lax.rem(chip + k, chips)
        spec_copy(j).wait_send()
        forward(j, lambda copy: copy.wait_send())
        solved_copy(j).wait_send()
        return 0

    forward(chip, lambda copy: copy.wait_send())
    lax.fori_loop(1, chips, drain_chips, 0)


def on_device(state, initial, forcing, kappa, reaction):
    steps, width, rows, depth = state.shape
    assert steps == 1
    members = lax.axis_size("tm")
    slabs = lax.axis_size("space")
    chips = members // 2
    half = width // 2
    total = width * rows
    piece = half * rows // chips
    ext = half + 2 * REACH
    dma = pltpu.SemaphoreType.DMA
    flat = lambda a: a.reshape(total, depth)
    padded = pltpu.VMEM((ext, rows + 16, depth), f32)
    wide = pltpu.VMEM((ext * rows, depth), f32)
    out = pl.pallas_call(
        functools.partial(kernel, members, slabs, width, rows),
        out_shape=jax.ShapeDtypeStruct((total, depth), bf16),
        in_specs=[pl.BlockSpec(memory_space=pltpu.HBM)] * 5,
        out_specs=pl.BlockSpec(memory_space=pltpu.VMEM),
        scratch_shapes=[
            *[pltpu.VMEM((total, depth), bf16)] * 5, dma((5,)),
            pltpu.VMEM((total, depth), bf16),
            pltpu.VMEM((2, 2 * rows, depth), bf16),
            pltpu.VMEM((3, ext * rows, depth), bf16),
            pltpu.VMEM((total, depth), bf16),
            pltpu.VMEM((members, piece, depth), bf16),
            pltpu.VMEM((chips, 2, piece, depth), bf16),
            pltpu.VMEM((2, ext * rows, depth), bf16),
            pltpu.VMEM((2, half * rows, depth), bf16),
            pltpu.VMEM((chips, 2, piece, depth), bf16),
            pltpu.VMEM((members, piece, depth), bf16),
            pltpu.VMEM((total, depth), bf16),
            wide, wide, wide, wide, wide,
            padded, padded, padded, padded,
            dma, dma, dma((2,)), dma((2,)), dma((4, 3)), dma((4, 3)),
            dma((members,)), dma((members,)), dma((chips,)), dma((chips,)),
            dma((4, chips)), dma((4, chips)), dma((chips,)), dma((chips,)), dma((members,)), dma((members,)),
        ],
        compiler_params=pltpu.CompilerParams(
            collective_id=0, has_side_effects=True, vmem_limit_bytes=40 * 2**20
        ),
    )(flat(state), flat(initial), flat(forcing), flat(kappa), flat(reaction))
    return out.reshape(state.shape)


def solution(mesh):
    cells = P("space", None, None)
    return jax.shard_map(
        on_device,
        mesh=mesh,
        in_specs=(P("tm", "space", None, None), cells, P("tm", "space", None, None), cells, cells),
        out_specs=P("tm", "space", None, None),
        check_vma=False,
    )
```

```python
import functools
import math

import jax
import jax.numpy as jnp
from jax import lax
from jax.experimental import pallas as pl
from jax.experimental.pallas import tpu as pltpu
from jax.sharding import PartitionSpec as P

SWEEPS = 6
ALPHA = 0.25
MESH = pl.DeviceIdType.MESH
f32, bf16 = jnp.float32, jnp.bfloat16
REACH = 2 * SWEEPS


def sweep_weights():
    return [1.0 / (1.0 + 0.4 * math.cos(math.pi * (2 * k + 1) / (2 * SWEEPS))) for k in range(SWEEPS)]


def pick(index, values):
    out = jnp.float32(values[0])
    for k in range(1, len(values)):
        out = jnp.where(index == k, jnp.float32(values[k]), out)
    return out


def scaled_sum(terms):
    total = None
    for factor, value in terms:
        if abs(factor) < 1e-12:
            continue
        if abs(factor - 1.0) < 1e-12:
            total = value if total is None else total + value
        elif abs(factor + 1.0) < 1e-12:
            total = -value if total is None else total - value
        else:
            part = value * jnp.float32(factor)
            total = part if total is None else total + part
    return total


def forward_transform(values):
    n = len(values)
    h = n // 2
    s = [v * jnp.float32(ALPHA ** (k / n)) if k else v for k, v in enumerate(values)]
    even = {k: s[k] + s[n - k] for k in range(1, h)}
    odd = {k: s[k] - s[n - k] for k in range(1, h)}
    even[0], even[h] = s[0], s[h]
    out = [None] * h
    ang = 2.0 * math.pi / n
    re = [None] * (h + 1)
    im = [None] * (h + 1)
    for j in range(h // 2 + 1):
        a = scaled_sum([(math.cos(ang * ((j * k) % n)), even[k]) for k in range(0, h + 1, 2)])
        b = scaled_sum([(math.cos(ang * ((j * k) % n)), even[k]) for k in range(1, h + 1, 2)])
        re[j] = a if b is None else a + b
        if h - j != j:
            re[h - j] = a if b is None else a - b
        if j:
            c = scaled_sum([(math.sin(ang * ((j * k) % n)), odd[k]) for k in range(2, h, 2)])
            d = scaled_sum([(math.sin(ang * ((j * k) % n)), odd[k]) for k in range(1, h, 2)])
            if h - j != j:
                im[j] = -(c + d)
                im[h - j] = c - d
            else:
                parts = [v for v in (c, d) if v is not None]
                im[j] = -sum(parts[1:], parts[0])
    out[0] = (re[0], re[h])
    for j in range(1, h):
        out[j] = (re[j], im[j])
    return out


def inverse_transform(pairs):
    h = len(pairs)
    n = 2 * h
    ang = 2.0 * math.pi / n
    x0, xh = pairs[0]
    re = {j: pairs[j][0] for j in range(1, h)}
    im = {j: pairs[j][1] for j in range(1, h)}
    q = h // 2
    rp = {j: re[j] + re[h - j] for j in range(1, q)}
    rm = {j: re[j] - re[h - j] for j in range(1, q)}
    ip = {j: im[j] + im[h - j] for j in range(1, q)}
    im_ = {j: im[j] - im[h - j] for j in range(1, q)}
    out = [None] * n
    s, d = x0 + xh, x0 - xh
    for k in range(h + 1):
        cos = lambda j: 2.0 * math.cos(ang * ((j * k) % n))
        sin = lambda j: 2.0 * math.sin(ang * ((j * k) % n))
        r = rp if k % 2 == 0 else rm
        i = im_ if k % 2 == 0 else ip
        c_part = scaled_sum([(cos(j), r[j]) for j in range(1, q)] + [(cos(q), re[q])])
        s_part = scaled_sum([(sin(j), i[j]) for j in range(1, q)] + [(sin(q), im[q])])
        base = s if k % 2 == 0 else d
        total = base if c_part is None else base + c_part
        scale = lambda m: jnp.float32(1.0 / (ALPHA ** (m / n) * n))
        if s_part is None:
            out[k] = total * scale(k)
            if 0 < k < h:
                out[n - k] = total * scale(n - k)
        else:
            out[k] = (total - s_part) * scale(k)
            if 0 < k < h:
                out[n - k] = (total + s_part) * scale(n - k)
    return out


def lane_sum(x, lane):
    depth = x.shape[-1]
    zero = jnp.zeros_like(x)
    near = jnp.where(lane >= 1, pltpu.roll(x, 1, 1), zero) + jnp.where(
        lane < depth - 1, pltpu.roll(x, depth - 1, 1), zero
    )
    far = jnp.where(lane >= 2, pltpu.roll(x, 2, 1), zero) + jnp.where(
        lane < depth - 2, pltpu.roll(x, depth - 2, 1), zero
    )
    return near, far


def neighbour_sum(ref, p, row, size, lane):
    c = ref[p, row : row + size, :]
    near, far = lane_sum(c, lane)
    near = near + (ref[p - 1, row : row + size, :] + ref[p + 1, row : row + size, :])
    far = far + (ref[p - 2, row : row + size, :] + ref[p + 2, row : row + size, :])
    near = near + (ref[p, row - 1 : row - 1 + size, :] + ref[p, row + 1 : row + 1 + size, :])
    far = far + (ref[p, row - 2 : row - 2 + size, :] + ref[p, row + 2 : row + 2 + size, :])
    return c, near * 0.5 + far


def around(ref, p, t, along):
    near = (ref[p - 1, t] + ref[p + 1, t]) + (ref[p, t - 1] + ref[p, t + 1])
    far = (ref[p - 2, t] + ref[p + 2, t]) + (ref[p, t - 2] + ref[p, t + 2])
    return ref[p, t], near * 0.5 + far + along


def split(x):
    high = x.astype(bf16)
    rest = x - high.astype(f32)
    mid = rest.astype(bf16)
    low = (rest - mid.astype(f32)).astype(bf16)
    return jnp.concatenate([high, mid, low], axis=1)


def put(ref, p, y, tiles, value, row):
    ref[p, y + 2] = value
    if y < 2:
        ref[p, y + 2 + tiles] = jnp.where(row < 7, pltpu.roll(value, 7, 0), jnp.zeros_like(value))
    if y >= tiles - 2:
        ref[p, y + 2 - tiles] = jnp.where(row >= 1, pltpu.roll(value, 1, 0), jnp.zeros_like(value))


def kernel(
    members, slabs, width, rows,
    state_h, initial_h, forcing_h, kappa_h, reaction_h, out,
    state, initial, forcing, kappa, reaction, load_s,
    prev, halo, cext, res, buf1, spec, tgt, sol, buf3, corr, buf4,
    ca, cc, ci, x0r, x0i, kp, pad_s, band, ar, ai, br, bi,
    prev_s, prev_r, halo_s, halo_r, coef_s, coef_r, s1, r1, s2, r2, sg, rg, s3, r3, s4, r4,
):
    chips = members // 2
    half = width // 2
    hr = half * rows
    piece = hr // chips
    ext = half + 2 * REACH
    extra = REACH - half
    depth = state.shape[1]
    me = lax.axis_index("tm")
    slab = lax.axis_index("space")
    chip = lax.div(me, 2)
    core = lax.rem(me, 2)
    part = slab * 2 + core
    parts = 2 * slabs
    chunks = [(r, 16) for r in range(0, rows, 16)]

    loads = [
        pltpu.make_async_copy(src, dst, load_s.at[k])
        for k, (src, dst) in enumerate((
            (state_h, state), (kappa_h, kappa), (reaction_h, reaction),
            (initial_h, initial), (forcing_h, forcing),
        ))
    ]
    for load in loads:
        load.start()

    barrier = pltpu.get_barrier_semaphore()

    def greet(k, _):
        other = lax.rem(me + k, members)
        pl.semaphore_signal(barrier, inc=1, device_id=(other, slab), device_id_type=MESH)
        return 0

    lax.fori_loop(1, members, greet, 0)
    has_low = slab > 0
    has_high = slab < slabs - 1
    for flag, step in ((has_low, -1), (has_high, 1)):
        @pl.when(flag)
        def _():
            for c in range(2):
                pl.semaphore_signal(
                    barrier, inc=1, device_id=(chip * 2 + c, slab + step), device_id_type=MESH
                )
    pad = jnp.zeros((8, depth), f32)

    def clear(p, _):
        pad_s[p, 0:8, :] = pad
        pad_s[p, 8 + rows : 16 + rows, :] = pad
        return 0

    lax.fori_loop(0, width + 4, clear, 0)
    pl.semaphore_wait(
        barrier,
        members - 1 + 2 * has_low.astype(jnp.int32) + 2 * has_high.astype(jnp.int32),
    )

    def remote(src, dst, send, recv, device):
        return pltpu.make_async_remote_copy(
            src_ref=src, dst_ref=dst, send_sem=send, recv_sem=recv,
            device_id=device, device_id_type=MESH,
        )

    def prev_copy():
        return remote(state, prev, prev_s, prev_r, (lax.rem(me + 1, members), slab))

    loads[0].wait()

    @pl.when(me < members - 1)
    def _():
        prev_copy().start()

    def halo_copy(side):
        src = state.at[pl.ds((width - 2) * rows, 2 * rows), :] if side == 0 else state.at[pl.ds(0, 2 * rows), :]
        return remote(src, halo.at[side], halo_s.at[side], halo_r.at[side],
                      (me, slab + (1 if side == 0 else -1)))

    sends = (has_high, has_low)
    gets = (has_low, has_high)
    for side in range(2):
        @pl.when(sends[side])
        def _():
            halo_copy(side).start()

        @pl.when(jnp.logical_not(gets[side]))
        def _():
            halo[side] = jnp.zeros((2 * rows, depth), bf16)

    moves = (
        (1, 0, half, REACH - half),
        (-1, 0, half, REACH + half),
        (2, half - extra, extra, 0),
        (-2, 0, extra, REACH + 2 * half),
    )

    def there(step):
        return jnp.logical_and(part + step >= 0, part + step < parts)

    def device_at(step):
        target = part + step
        return (chip * 2 + lax.rem(target + 2, 2), lax.div(target + 2, 2) - 1)

    coefs = (kappa, reaction, initial)

    def coef_copy(m, a):
        step, first, count, place = moves[m]
        src = coefs[a].at[pl.ds(pl.multiple_of(core * hr + first * rows, 16), count * rows), :]
        return remote(src, cext.at[a, pl.ds(place * rows, count * rows), :],
                      coef_s.at[m, a], coef_r.at[m, a], device_at(step))

    for load in loads[1:4]:
        load.wait()
    for m, (step, first, count, place) in enumerate(moves):
        @pl.when(there(step))
        def _():
            for a in range(3):
                coef_copy(m, a).start()

        @pl.when(jnp.logical_not(there(-step)))
        def _():
            for a in range(3):
                cext[a, pl.ds(place * rows, count * rows), :] = jnp.zeros((count * rows, depth), bf16)
            for a in range(2):
                tgt[a, pl.ds(place * rows, count * rows), :] = jnp.zeros((count * rows, depth), bf16)

    for a in range(3):
        cext[a, pl.ds(REACH * rows, hr), :] = coefs[a][pl.ds(pl.multiple_of(core * hr, 16), hr), :]

    lane = lax.broadcasted_iota(jnp.int32, (16, depth), 1)
    apart = jnp.abs(
        lax.broadcasted_iota(jnp.int32, (depth, depth), 0)
        - lax.broadcasted_iota(jnp.int32, (depth, depth), 1)
    )
    taps = jnp.where(apart == 1, 0.5, jnp.where(apart == 2, 1.0, 0.0)).astype(bf16)
    for k in range(3):
        band[k * depth : (k + 1) * depth, :] = taps
    row8 = lax.broadcasted_iota(jnp.int32, (8, depth), 0)
    tiles = rows // 8

    def strided(ref, p, y):
        first = pl.multiple_of(p * rows, 16)
        return jnp.concatenate([ref[pl.ds(first + y + d, 8, stride=tiles), :] for d in range(2)], axis=0)

    def widen(p, _):
        for r, n in chunks:
            at = pl.ds(pl.multiple_of(p * rows, 16) + r, n)
            pad_s[p + 2, 8 + r : 8 + r + n, :] = state[at, :].astype(f32)
        return 0

    lax.fori_loop(0, width, widen, 0)
    for side in range(2):
        @pl.when(gets[side])
        def _():
            halo_copy(side).wait_recv()
        for p in range(2):
            at = p if side == 0 else width + 2 + p
            pad_s[at, 8 : 8 + rows, :] = halo[side, p * rows : (p + 1) * rows, :].astype(f32)

    loads[4].wait()

    @pl.when(me == 0)
    def _():
        prev[...] = initial[...]

    @pl.when(me > 0)
    def _():
        prev_copy().wait_recv()

    def piece_copy(i):
        owner = 2 * lax.rem(i, chips) + lax.div(i, chips)
        return owner, remote(res.at[pl.ds(pl.multiple_of(i * piece, 16), piece), :], buf1.at[me],
                             s1.at[i], r1.at[me], (owner, slab))

    per_plane = rows // piece

    def residual_plane(k, _):
        p = lax.rem(k + core * half + lax.div(chip, per_plane) + 1, width)
        for r, n in chunks:
            at = pl.ds(pl.multiple_of(p * rows, 16) + r, n)
            c, total = neighbour_sum(pad_s, p + 2, 8 + r, n, lane)
            kap = kappa[at, :].astype(f32)
            value = (
                forcing[at, :].astype(f32) - c + prev[at, :].astype(f32)
                - kap * (9.0 * c - total)
                - reaction[at, :].astype(f32) * c * c * c
            )
            x0r[at, :] = value
        for y in range(0, tiles, 2):
            to = pl.ds(pl.multiple_of(p * rows, 16) + 8 * y, 16)
            res[to, :] = strided(x0r, p, y).astype(bf16)
        for sub in range(per_plane):
            i = p * per_plane + sub
            owner, copy = piece_copy(i)

            @pl.when(owner != me)
            def _():
                copy.start()
        return 0

    lax.fori_loop(0, width, residual_plane, 0)
    mine = core * chips + chip
    buf1[me] = res[pl.ds(pl.multiple_of(mine * piece, 16), piece), :]

    def wait_1(n, _):
        @pl.when(n != me)
        def _():
            remote(res.at[pl.ds(0, piece), :], buf1.at[n], s1.at[0], r1.at[n], (me, slab)).wait_recv()
        return 0

    lax.fori_loop(0, members, wait_1, 0)

    def transform(t, _):
        at = pl.ds(pl.multiple_of(t * 16, 16), 16)
        pairs = forward_transform([buf1[n, at, :].astype(f32) for n in range(members)])
        for j in range(chips):
            spec[j, 0, at, :] = pairs[j][0].astype(bf16)
            spec[j, 1, at, :] = pairs[j][1].astype(bf16)
        return 0

    lax.fori_loop(0, piece // 16, transform, 0)

    def my_rows(first):
        return pl.ds(pl.multiple_of(first * rows + chip * piece, 16), piece)

    def spec_copy(j):
        return remote(spec.at[j], tgt.at[:, my_rows(REACH), :], s2.at[j], r2.at[chip],
                      (2 * j + core, slab))

    def send_2(k, _):
        spec_copy(lax.rem(chip + k, chips)).start()
        return 0

    lax.fori_loop(1, chips, send_2, 0)
    tgt[:, my_rows(REACH), :] = spec[chip]

    def forward(j, action):
        at = j * piece
        for m, (step, first, count, place) in enumerate(moves):
            inside = jnp.logical_and(at >= first * rows, at < (first + count) * rows)

            @pl.when(jnp.logical_and(there(step), inside))
            def _():
                target = pl.multiple_of(place * rows + at - first * rows, 16)
                copy = remote(
                    tgt.at[:, pl.ds(pl.multiple_of(REACH * rows + at, 16), piece), :],
                    tgt.at[:, pl.ds(target, piece), :],
                    sg.at[m, j], rg.at[m, j], device_at(step))
                action(copy)

    def arrived(m, j):
        step, first, count, place = moves[m]
        at = j * piece
        inside = jnp.logical_and(at >= first * rows, at < (first + count) * rows)

        @pl.when(jnp.logical_and(there(-step), inside))
        def _():
            target = pl.multiple_of(place * rows + at - first * rows, 16)
            remote(
                tgt.at[:, pl.ds(REACH * rows, piece), :],
                tgt.at[:, pl.ds(target, piece), :],
                sg.at[m, j], rg.at[m, j], (me, slab)).wait_recv()

    forward(chip, lambda copy: copy.start())

    def wait_2(k, _):
        j = lax.rem(chip + chips - k, chips)
        remote(spec.at[0], tgt.at[:, pl.ds(pl.multiple_of(REACH * rows + j * piece, 16), piece), :],
               s2.at[0], r2.at[j], (me, slab)).wait_recv()
        forward(j, lambda copy: copy.start())
        return 0

    lax.fori_loop(1, chips, wait_2, 0)

    for m, (step, first, count, place) in enumerate(moves):
        @pl.when(there(-step))
        def _():
            for a in range(3):
                coef_copy(m, a).wait_recv()

    b = ALPHA ** (1.0 / members)
    ang = 2.0 * math.pi / members
    shift_a = pick(chip, [1.0 - b * math.cos(ang * j) for j in range(chips)])
    shift_c = pick(chip, [1.0 + b] + [1.0 - b * math.cos(ang * j) for j in range(1, chips)])
    shift_i = pick(chip, [0.0] + [b * math.sin(ang * j) for j in range(1, chips)])

    def coefficients(p, _):
        for r, n in chunks:
            at = pl.ds(pl.multiple_of(p * rows, 16) + r, n)
            kap = cext[0, at, :].astype(f32)
            ini = cext[2, at, :].astype(f32)
            x0r[at, :] = kap
            x0i[at, :] = 9.0 * kap + 3.0 * cext[1, at, :].astype(f32) * ini * ini
        for y in range(0, tiles, 2):
            at = pl.ds(pl.multiple_of(p * rows, 16) + 8 * y, 16)
            base = strided(x0i, p, y)
            da = shift_a + base
            dc = shift_c + base
            ia = 1.0 / (da * da + shift_i * shift_i)
            ic = 1.0 / (dc * dc + shift_i * shift_i)
            kp[at, :] = strided(x0r, p, y)
            ca[at, :] = da * ia
            cc[at, :] = dc * ic
            ci[at, :] = shift_i * ia
        return 0

    lax.fori_loop(0, ext, coefficients, 0)

    def opening(p, _):
        for r, n in chunks:
            at = pl.ds(pl.multiple_of(p * rows, 16) + r, n)
            yr = tgt[0, at, :].astype(f32)
            yi = tgt[1, at, :].astype(f32)
            kap = kp[at, :]
            a, c, i = ca[at, :], cc[at, :], ci[at, :]
            xr = yr * a + yi * i
            xi = yi * c - yr * i
            x0r[at, :] = xr
            x0i[at, :] = xi
            for d in range(2):
                put(ar, p, r // 8 + d, tiles, xr[8 * d : 8 * d + 8, :], row8)
                put(ai, p, r // 8 + d, tiles, xi[8 * d : 8 * d + 8, :], row8)
            ca[at, :] = a * kap
            cc[at, :] = c * kap
            ci[at, :] = i * kap
        return 0

    lax.fori_loop(REACH, REACH + half, opening, 0)
    def arrivals(k, _):
        j = lax.rem(chip + chips - k, chips)
        for m in range(4):
            arrived(m, j)
        return 0

    lax.fori_loop(0, chips, arrivals, 0)
    lax.fori_loop(0, REACH, opening, 0)
    lax.fori_loop(REACH + half, ext, opening, 0)

    def solved_copy(j):
        return remote(sol.at[:, pl.ds(pl.multiple_of(j * piece, 16), piece), :], buf3.at[chip],
                      s3.at[j], r3.at[chip], (2 * j + core, slab))

    weights = sweep_weights()
    for k in range(SWEEPS):
        sr, si, dr, di = (ar, ai, br, bi) if k % 2 == 0 else (br, bi, ar, ai)
        w = weights[k]
        last = k == SWEEPS - 1

        def sweep(turn, _):
            p0 = 2 * k + 2 + 4 * turn
            if last:
                p0 = REACH + lax.rem(4 * turn + 4 * lax.div(lax.div(chip, per_plane) + 1, 4), half)
            lifted = [
                ref[p0 + e, 2 : 2 + tiles].reshape(rows, depth) for e in range(4) for ref in (sr, si)
            ]
            along = jnp.dot(
                split(jnp.concatenate(lifted, axis=0)), band[...], preferred_element_type=f32
            )
            for e in range(4):
                p = p0 + e
                solved = []
                for y in range(tiles):
                    at = pl.ds(pl.multiple_of(p * rows, 16) + 8 * y, 8)
                    first = 2 * e * rows + 8 * y
                    xr, tr = around(sr, p, y + 2, along[first : first + 8, :])
                    xi, ti = around(si, p, y + 2, along[first + rows : first + rows + 8, :])
                    i = ci[at, :]
                    nr = (x0r[at, :] + ca[at, :] * tr + i * ti) * w + xr * (1.0 - w)
                    ni = (x0i[at, :] + cc[at, :] * ti - i * tr) * w + xi * (1.0 - w)
                    if last:
                        solved.append((nr, ni))
                        if y % 2:
                            to = pl.ds(pl.multiple_of((p - REACH) * rows, 16) + 8 * y - 8, 16)
                            for k2 in range(2):
                                both = jnp.concatenate([solved[y - 1][k2], solved[y][k2]], axis=0)
                                sol[k2, to, :] = both.astype(bf16)
                    else:
                        put(dr, p, y, tiles, nr, row8)
                        put(di, p, y, tiles, ni, row8)
                if last:
                    for sub in range(per_plane):
                        j = (p - REACH) * per_plane + sub

                        @pl.when(j != chip)
                        def _():
                            solved_copy(j).start()
            return 0

        lax.fori_loop(0, (ext - 4 * k - 4) // 4, sweep, 0)

    buf3[chip] = sol[:, my_rows(0), :]

    def wait_3(k, _):
        j = lax.rem(chip + k, chips)
        remote(sol.at[:, pl.ds(0, piece), :], buf3.at[j], s3.at[0], r3.at[j], (me, slab)).wait_recv()
        return 0

    lax.fori_loop(1, chips, wait_3, 0)

    def back(t, _):
        at = pl.ds(pl.multiple_of(t * 16, 16), 16)
        pairs = [(buf3[j, 0, at, :].astype(f32), buf3[j, 1, at, :].astype(f32)) for j in range(chips)]
        for n, value in enumerate(inverse_transform(pairs)):
            corr[n, at, :] = value.astype(bf16)
        return 0

    lax.fori_loop(0, piece // 16, back, 0)
    here = pl.ds(pl.multiple_of(mine * piece, 16), piece)

    def send_4(k, _):
        n = lax.rem(me + k, members)
        remote(corr.at[n], buf4.at[here, :], s4.at[n], r4.at[mine], (n, slab)).start()
        return 0

    lax.fori_loop(1, members, send_4, 0)
    buf4[here, :] = corr[me]

    def wait_4(i, _):
        @pl.when(i != mine)
        def _():
            remote(corr.at[0], buf4.at[pl.ds(pl.multiple_of(i * piece, 16), piece), :],
                   s4.at[0], r4.at[i], (me, slab)).wait_recv()
        return 0

    lax.fori_loop(0, members, wait_4, 0)

    def finish(p, _):
        first = pl.multiple_of(p * rows, 16)
        for r, n in chunks:
            at = pl.ds(first + r, n)
            x0r[at, :] = buf4[at, :].astype(f32)
        for g in range(0, 8, 2):
            at = pl.ds(first + g * tiles, 2 * tiles)
            natural = jnp.concatenate(
                [x0r[pl.ds(first + g + d, tiles, stride=8), :] for d in range(2)], axis=0
            )
            out[at, :] = (state[at, :].astype(f32) + natural).astype(bf16)
        return 0

    lax.fori_loop(0, width, finish, 0)

    @pl.when(me < members - 1)
    def _():
        prev_copy().wait_send()

    for side in range(2):
        @pl.when(sends[side])
        def _():
            halo_copy(side).wait_send()
    for m, (step, first, count, place) in enumerate(moves):
        @pl.when(there(step))
        def _():
            for a in range(3):
                coef_copy(m, a).wait_send()

    def drain_members(n, _):
        owner, copy = piece_copy(n)

        @pl.when(owner != me)
        def _():
            copy.wait_send()

        @pl.when(n != me)
        def _():
            remote(corr.at[n], buf4.at[here, :], s4.at[n], r4.at[mine], (n, slab)).wait_send()
        return 0

    lax.fori_loop(0, members, drain_members, 0)

    def drain_chips(k, _):
        j = lax.rem(chip + k, chips)
        spec_copy(j).wait_send()
        forward(j, lambda copy: copy.wait_send())
        solved_copy(j).wait_send()
        return 0

    forward(chip, lambda copy: copy.wait_send())
    lax.fori_loop(1, chips, drain_chips, 0)


def on_device(state, initial, forcing, kappa, reaction):
    steps, width, rows, depth = state.shape
    assert steps == 1
    members = lax.axis_size("tm")
    slabs = lax.axis_size("space")
    chips = members // 2
    half = width // 2
    total = width * rows
    piece = half * rows // chips
    ext = half + 2 * REACH
    dma = pltpu.SemaphoreType.DMA
    flat = lambda a: a.reshape(total, depth)
    padded = pltpu.VMEM((ext, rows // 8 + 4, 8, depth), f32)
    wide = pltpu.VMEM((ext * rows, depth), f32)
    out = pl.pallas_call(
        functools.partial(kernel, members, slabs, width, rows),
        out_shape=jax.ShapeDtypeStruct((total, depth), bf16),
        in_specs=[pl.BlockSpec(memory_space=pltpu.HBM)] * 5,
        out_specs=pl.BlockSpec(memory_space=pltpu.VMEM),
        scratch_shapes=[
            *[pltpu.VMEM((total, depth), bf16)] * 5, dma((5,)),
            pltpu.VMEM((total, depth), bf16),
            pltpu.VMEM((2, 2 * rows, depth), bf16),
            pltpu.VMEM((3, ext * rows, depth), bf16),
            pltpu.VMEM((total, depth), bf16),
            pltpu.VMEM((members, piece, depth), bf16),
            pltpu.VMEM((chips, 2, piece, depth), bf16),
            pltpu.VMEM((2, ext * rows, depth), bf16),
            pltpu.VMEM((2, half * rows, depth), bf16),
            pltpu.VMEM((chips, 2, piece, depth), bf16),
            pltpu.VMEM((members, piece, depth), bf16),
            pltpu.VMEM((total, depth), bf16),
            wide, wide, wide, wide, wide, wide,
            pltpu.VMEM((width + 4, rows + 16, depth), f32), pltpu.VMEM((3 * depth, depth), bf16),
            padded, padded, padded, padded,
            dma, dma, dma((2,)), dma((2,)), dma((4, 3)), dma((4, 3)),
            dma((members,)), dma((members,)), dma((chips,)), dma((chips,)),
            dma((4, chips)), dma((4, chips)), dma((chips,)), dma((chips,)), dma((members,)), dma((members,)),
        ],
        compiler_params=pltpu.CompilerParams(
            collective_id=0, has_side_effects=True, vmem_limit_bytes=40 * 2**20
        ),
    )(flat(state), flat(initial), flat(forcing), flat(kappa), flat(reaction))
    return out.reshape(state.shape)


def solution(mesh):
    cells = P("space", None, None)
    return jax.shard_map(
        on_device,
        mesh=mesh,
        in_specs=(P("tm", "space", None, None), cells, P("tm", "space", None, None), cells, cells),
        out_specs=P("tm", "space", None, None),
        check_vma=False,
    )
```
